32 devices in a mesh: groups: 2 (over x), batch: 4 (over z), mp: 4 (over y, core).
Axes of the slice: x: 2, y: 2, z: 4, core: 2. Of those that a mesh axis runs over, the one named last changes fastest.
Arguments:
- queries: bfloat16 [32, 32, 4096], P(('groups', 'batch'), None, 'mp'), parts along dimension 0, may hold values from -8 to 8
- prefix_key_cache: bfloat16 [32, 4096, 512], P(('groups', 'batch'), 'mp'), parts along dimension 0, may hold values from -8 to 8
- prefix_value_cache: bfloat16 [32, 4096, 512], P(('groups', 'batch'), 'mp'), parts along dimension 0, may hold values from -6 to 6
- tree_node_keys: bfloat16 [32, 32, 512], P(('groups', 'batch')), parts along dimension 0, may hold values from -8 to 8
- tree_node_values: bfloat16 [32, 32, 512], P(('groups', 'batch')), parts along dimension 0, may hold values from -6 to 6
- lengths: int32 [32], P(('groups', 'batch')), parts along dimension 0, may hold values from 1024 to 4096, as said below
- parents: int32 [32, 32], P(('groups', 'batch')), parts along dimension 0, may hold values from 0 to 30, as said below
- request_adapter_index: int32 [32], P('groups'), parts along dimension 0, may hold values from 0 to 15, as said below
- output_projection_weight: bfloat16 [4096, 8192], P('mp'), may hold values from -0.23925781 to 0.23925781
- adapter_down_weight: bfloat16 [16, 64, 4096], P('batch', None, 'mp'), may hold values from -0.09375 to 0.09375
- adapter_up_weight: bfloat16 [16, 64, 8192], P('batch', None, 'mp'), may hold values from -0.75 to 0.75
Outputs:
- block_output: bfloat16 [32, 32, 8192], P(('groups', 'batch'), None, 'mp'), parts along dimension 0
The draws below stay inside these ranges and needn't reach their ends.
There are 2 independent parts, one for each index of `groups`. The reference program is written for one: setup_inputs(seed, part) draws one part's arguments, and reference() takes and returns one part's arrays. A program takes and returns all parts, laid end to end along the dimension named above; an argument that names none is the same for every part. Nothing has to cross between parts.
Inputs may be any that keep to these rules, and one draw needn't show every extreme that they name: `lengths`: at least 2; one request of every draw has a prefix of exactly 4096. parents[r, 0] = 0 and parents[r, i] < i for i >= 1. `request_adapter_index`: adapter a is held by batch index a // 4; among the 4 requests of one batch index (requests b * 4 to b * 4 + 3) at most 2 use adapters held by one batch index, and in every such block one batch index serves exactly 2.
All inputs are finite; a program needn't handle non-finite values.
Results may differ from the reference program's by a relative error of at most 0.022.
Values may be sent and summed in bfloat16 or wider, within the bound.
A program may use at most 128 MiB of HBM per device.

```python
import jax
import jax.numpy as jnp
from jax import lax

MODEL_WIDTH = 8192
QUERY_HEADS = 32
KVH = 4
HEAD_WIDTH = 128
ADAPTER_RANK = 64
NODES = 32
REQ_DEV = 4
ADP_DEV = 4
CAP = 2
REQ = 16
PREFIX = 4096
ADAPTER_POOL = 16
N_MP = 4


def draw_queries(key, part):
    key = jax.random.fold_in(key, 3)
    array_shape = (REQ, NODES, KVH, QUERY_HEADS // KVH, HEAD_WIDTH)
    base = jnp.clip(2.0 * jax.random.normal(key, array_shape, jnp.float32), -8.0, 8.0)
    return base.reshape(REQ, NODES, QUERY_HEADS * HEAD_WIDTH).astype(jnp.bfloat16)


def draw_prefix_key_cache(key, part):
    key = jax.random.fold_in(key, 5)
    array_shape = (REQ, PREFIX, KVH, HEAD_WIDTH)
    base = jnp.clip(jax.random.normal(key, array_shape, jnp.float32), -8.0, 8.0)
    return base.reshape(REQ, PREFIX, KVH * HEAD_WIDTH).astype(jnp.bfloat16)


def draw_lengths(key, part):
    key = jax.random.fold_in(key, 7)
    key_vals, key_full = jax.random.split(key)
    values = jax.random.randint(key_vals, (REQ,), PREFIX // 4, PREFIX + 1)
    full_at = jax.random.randint(key_full, (), 0, REQ)
    return jnp.where(jnp.arange(REQ) == full_at, PREFIX, values).astype(jnp.int32)


def draw_parents(key, part):
    key = jax.random.fold_in(key, 9)
    upper = jnp.maximum(jnp.arange(NODES, dtype=jnp.int32), 1)
    return jax.random.randint(key, (REQ, NODES), 0, upper[None, :]).astype(jnp.int32)


def draw_request_adapter_index(key, part):
    key = jax.random.fold_in(key, 11)
    blocks = REQ // REQ_DEV
    key_hot, key_fill, key_local = jax.random.split(key, 3)
    hot_owner = jax.random.randint(key_hot, (), 0, blocks)
    others = jnp.repeat(jnp.arange(blocks - 1, dtype=jnp.int32), CAP)
    others = others + (others >= hot_owner).astype(jnp.int32)

    def one_block(block_key):
        key_pick, key_order = jax.random.split(block_key)
        picked = jax.random.permutation(key_pick, others)[:REQ_DEV - CAP]
        owners = jnp.concatenate([jnp.full((CAP,), hot_owner, jnp.int32), picked])
        return jax.random.permutation(key_order, owners)
    owner_rows = jax.vmap(one_block)(jax.random.split(key_fill, blocks))
    local_ids = jax.random.randint(key_local, (blocks, REQ_DEV), 0, ADP_DEV)
    return (owner_rows * ADP_DEV + local_ids).reshape(REQ).astype(jnp.int32)


def with_spikes(drawn, key, source, target, parts, factor):
    def block_of(axis_at):
        return (jnp.arange(drawn.shape[axis_at]) // (drawn.shape[axis_at] // parts)).reshape((-1,) + (1,) * (drawn.ndim - 1 - axis_at))

    first = jax.random.permutation(key, parts)[block_of(target)]
    second = (block_of(target) + parts // 2) % parts
    return jnp.where((block_of(source) == first) | (block_of(source) == second), factor * drawn, drawn)


def block_levels(rng, shape, pieces, low, high):
    loudness, own = 1.0, jax.random.fold_in(rng, 6)
    for axis_at, blocks in pieces:
        draws = jnp.exp(jax.random.uniform(jax.random.fold_in(own, axis_at), (blocks,), jnp.float32, low / len(pieces), high / len(pieces)))
        loudness = loudness * jnp.repeat(draws, shape[axis_at] // blocks).reshape([-1 if axis == axis_at else 1 for axis in range(len(shape))])
    return loudness


def centred(key, shape, deviation, bound, shards=(), held_as=jnp.bfloat16):
    values = deviation * jax.random.normal(key, shape, jnp.float32)
    if shards:
        values = values * block_levels(key, shape, shards, -0.22, 0.18)
    return jnp.clip(values, -bound, bound).astype(held_as)


def noise_with(rng, shape, deviation, reach, pieces, heavy, kind=jnp.bfloat16):
    result = deviation * jax.random.normal(rng, shape, jnp.float32)
    if pieces:
        result = result * block_levels(rng, shape, pieces, -0.22, 0.18)
    return jnp.clip(with_spikes(result, jax.random.fold_in(rng, 3), *heavy), -reach, reach).astype(kind)


def setup_inputs(seed: int = 0, part: int = 0) -> dict:
    seeds = jax.random.split(jax.random.key(seed), 12)
    part_keys = jax.random.split(jax.random.fold_in(seeds[11], part), 12)
    queries = draw_queries(jax.random.fold_in(jax.random.fold_in(seeds[11], part), 71), part)
    prefix_key_cache = draw_prefix_key_cache(jax.random.fold_in(jax.random.fold_in(seeds[11], part), 71), part)
    prefix_value_cache = centred(part_keys[2], (REQ, PREFIX, KVH * HEAD_WIDTH), 1.0, 6.0, ((0, 4), (1, 4)))
    tree_node_keys = centred(part_keys[3], (REQ, NODES, KVH * HEAD_WIDTH), 2.0, 8.0, ((0, 4),))
    tree_node_values = centred(part_keys[4], (REQ, NODES, KVH * HEAD_WIDTH), 1.0, 6.0, ((0, 4),))
    lengths = draw_lengths(jax.random.fold_in(jax.random.fold_in(seeds[11], part), 71), part)
    parents = draw_parents(jax.random.fold_in(jax.random.fold_in(seeds[11], part), 71), part)
    request_adapter_index = draw_request_adapter_index(jax.random.fold_in(jax.random.fold_in(seeds[11], part), 71), part)
    output_projection_weight = noise_with(seeds[8], (QUERY_HEADS * HEAD_WIDTH, MODEL_WIDTH), 0.04, 0.23925781, ((0, 4),), (0, 1, 4, 2.0))
    adapter_down_weight = centred(seeds[9], (ADAPTER_POOL, ADAPTER_RANK, QUERY_HEADS * HEAD_WIDTH), (QUERY_HEADS * HEAD_WIDTH) ** -0.5, 0.09375, ((0, 4), (2, 4)))
    adapter_up_weight = centred(seeds[10], (ADAPTER_POOL, ADAPTER_RANK, MODEL_WIDTH), ADAPTER_RANK ** -0.5, 0.75, ((0, 4), (2, 4)))
    return {"queries": queries, "prefix_key_cache": prefix_key_cache, "prefix_value_cache": prefix_value_cache, "tree_node_keys": tree_node_keys, "tree_node_values": tree_node_values, "lengths": lengths, "parents": parents, "request_adapter_index": request_adapter_index, "output_projection_weight": output_projection_weight, "adapter_down_weight": adapter_down_weight, "adapter_up_weight": adapter_up_weight}


NEG_FILL = -1e+30
ADAPTER_SCALE = 2.0

def ancestors(parents):
    tree_node_count = parents.shape[-1]
    identity_mat = jnp.eye(tree_node_count, dtype=jnp.float32)
    parent_mat = (parents[..., :, None] == jnp.arange(tree_node_count, dtype=jnp.int32)[None, :]).astype(jnp.float32)
    reached = jnp.minimum(identity_mat + parent_mat, 1.0)
    for repeat in range(max(1, (tree_node_count - 1).bit_length())):
        reached = jnp.minimum(jnp.matmul(reached, reached, precision=lax.Precision.HIGHEST), 1.0)
    return reached > 0.5

def reference(queries, prefix_key_cache, prefix_value_cache, tree_node_keys, tree_node_values, lengths, parents, request_adapter_index, output_projection_weight, adapter_down_weight, adapter_up_weight):
    group_size = QUERY_HEADS // KVH
    inv_root = 1.0 / jnp.sqrt(jnp.float32(HEAD_WIDTH))
    linked_all = ancestors(parents)

    def attend_one(inputs):
        query_row, keys_row, values_row, tkeys_row, tvalues_row, length_one, linked = inputs
        query_blocks = query_row.reshape(NODES, KVH, group_size, HEAD_WIDTH).astype(jnp.float32)
        key_blocks = keys_row.reshape(PREFIX, KVH, HEAD_WIDTH).astype(jnp.float32)
        value_blocks = values_row.reshape(PREFIX, KVH, HEAD_WIDTH).astype(jnp.float32)
        tkey_blocks = tkeys_row.reshape(NODES, KVH, HEAD_WIDTH).astype(jnp.float32)
        tvalue_blocks = tvalues_row.reshape(NODES, KVH, HEAD_WIDTH).astype(jnp.float32)
        scores = jnp.einsum('ngid,pgd->ngip', query_blocks, key_blocks) * inv_root
        tree_scores = jnp.einsum('ngid,mgd->ngim', query_blocks, tkey_blocks) * inv_root
        valid = (jnp.arange(PREFIX, dtype=jnp.int32) < length_one)[None, None, None, :]
        tree_valid = linked[:, None, None, :]
        top_value = jnp.maximum(lax.optimization_barrier(jnp.max(jnp.where(valid, scores, NEG_FILL), axis=-1)), lax.optimization_barrier(jnp.max(jnp.where(tree_valid, tree_scores, NEG_FILL), axis=-1)))
        weights = jnp.where(valid, jnp.exp(scores - top_value[..., None]), 0.0)
        tree_w = jnp.where(tree_valid, jnp.exp(tree_scores - top_value[..., None]), 0.0)
        total = lax.optimization_barrier(jnp.sum(weights, axis=-1)) + lax.optimization_barrier(jnp.sum(tree_w, axis=-1))
        numerator = jnp.einsum('ngip,pgd->ngid', weights.astype(jnp.bfloat16).astype(jnp.float32), value_blocks)
        numerator = numerator + jnp.einsum('ngim,mgd->ngid', tree_w.astype(jnp.bfloat16).astype(jnp.float32), tvalue_blocks)
        return (numerator / total[..., None]).reshape(NODES, QUERY_HEADS * HEAD_WIDTH).astype(jnp.bfloat16)
    attended = lax.map(attend_one, (queries, prefix_key_cache, prefix_value_cache, tree_node_keys, tree_node_values, lengths, linked_all))
    heads_here = QUERY_HEADS // N_MP
    attn_blocks = attended.reshape(REQ * NODES, N_MP, heads_here * HEAD_WIDTH)
    weight_blocks = output_projection_weight.reshape(N_MP, heads_here * HEAD_WIDTH, MODEL_WIDTH)

    def add_block(carry, index):
        piece = jnp.dot(attn_blocks[:, index], weight_blocks[index], preferred_element_type=jnp.float32).astype(jnp.bfloat16)
        piece = lax.optimization_barrier(piece)
        return (carry + piece.astype(jnp.float32), None)
    projected_output, unused = lax.scan(add_block, jnp.zeros((REQ * NODES, MODEL_WIDTH), jnp.float32), jnp.arange(N_MP, dtype=jnp.int32))
    projected_output = projected_output.reshape(REQ, NODES, MODEL_WIDTH)

    def adapt_one(inputs):
        attn_row, identity_matrix = inputs
        down_matrix = adapter_down_weight[identity_matrix]
        up_matrix = adapter_up_weight[identity_matrix]
        shrunk = jnp.dot(attn_row, down_matrix.T, preferred_element_type=jnp.float32).astype(jnp.bfloat16)
        return jnp.dot(shrunk, up_matrix, preferred_element_type=jnp.float32)
    raised_output = lax.map(adapt_one, (attended, request_adapter_index))
    return (projected_output + ADAPTER_SCALE * raised_output).astype(jnp.bfloat16)
```

```python
import functools
import math

import jax
import jax.numpy as jnp
from jax import lax
from jax.experimental import pallas as pl
from jax.experimental.pallas import tpu as pltpu
from jax.sharding import PartitionSpec as P

HEAD_WIDTH = 128
ADAPTER_RANK = 64
CAP = 2
LANES = 128
NEG_FILL = -1e30
ADAPTER_SCALE = 2.0
INV_ROOT = 1.0 / math.sqrt(HEAD_WIDTH)
VMEM_LIMIT = 48 << 20
CONTRACT_LAST = (((1,), (1,)), ((), ()))
CONTRACT_INNER = (((1,), (0,)), ((), ()))


def dot(a, b, dims=CONTRACT_INNER):
    return lax.dot_general(a, b, dims, preferred_element_type=jnp.float32)


def params(**more):
    return pltpu.CompilerParams(vmem_limit_bytes=VMEM_LIMIT, **more)


def ancestors(parents):
    tree_node_count = parents.shape[-1]
    identity_mat = jnp.eye(tree_node_count, dtype=jnp.float32)
    parent_mat = (
        parents[..., :, None] == jnp.arange(tree_node_count, dtype=jnp.int32)[None, :]
    ).astype(jnp.float32)
    reached = jnp.minimum(identity_mat + parent_mat, 1.0)
    for repeat in range(max(1, (tree_node_count - 1).bit_length())):
        step = reached.astype(jnp.bfloat16)
        reached = jnp.minimum(
            jnp.einsum("rnm,rmk->rnk", step, step, preferred_element_type=jnp.float32), 1.0
        )
    return reached


def pick_kernel(picked_ref, down_ref, up_ref, down_out, up_out):
    down_out[...] = down_ref[...]
    up_out[...] = up_ref[...]


def pick(picked, down, up):
    slots = picked.shape[0]
    present, rank, width = down.shape
    up_width = up.shape[2]
    return pl.pallas_call(
        pick_kernel,
        grid_spec=pltpu.PrefetchScalarGridSpec(
            num_scalar_prefetch=1,
            grid=(slots,),
            in_specs=[
                pl.BlockSpec((1, rank, width), lambda s, p: (p[s], 0, 0)),
                pl.BlockSpec((1, rank, up_width), lambda s, p: (p[s], 0, 0)),
            ],
            out_specs=[
                pl.BlockSpec((1, rank, width), lambda s, p: (s, 0, 0)),
                pl.BlockSpec((1, rank, up_width), lambda s, p: (s, 0, 0)),
            ],
        ),
        out_shape=[
            jax.ShapeDtypeStruct((slots, rank, width), down.dtype),
            jax.ShapeDtypeStruct((slots, rank, up_width), up.dtype),
        ],
        compiler_params=params(),
        name="pick",
    )(picked, down, up)


def attend_kernel(group_size, meta_ref, q_ref, k_ref, v_ref, out_ref):
    blocks, _, nodes, width_here = q_ref.shape
    heads_here = width_here // HEAD_WIDTH
    request = pl.program_id(0)
    positions = k_ref.shape[1]
    left = meta_ref[request]
    rows = []
    for block in range(blocks):
        for head in range(heads_here):
            rows.append(q_ref[block, 0, :, head * HEAD_WIDTH : (head + 1) * HEAD_WIDTH])
    query = jnp.concatenate(rows, axis=0)
    scores = dot(query, k_ref[0], CONTRACT_LAST) * INV_ROOT
    place = lax.broadcasted_iota(jnp.int32, (1, positions), 1)
    valid = place < left
    scores = jnp.where(valid, scores, NEG_FILL)
    top = jnp.max(scores, axis=1, keepdims=True).astype(jnp.bfloat16).astype(jnp.float32)
    weights = jnp.where(valid, jnp.exp(scores - top), 0.0)
    total = jnp.sum(weights, axis=1, keepdims=True)
    summed = dot(weights.astype(jnp.bfloat16), v_ref[0]).astype(jnp.bfloat16)
    high = total.astype(jnp.bfloat16).astype(jnp.float32)
    low = total - high
    lane = lax.broadcasted_iota(jnp.int32, (nodes, LANES), 1)
    for block in range(blocks):
        stats = jnp.zeros((nodes, LANES), jnp.float32)
        for head in range(heads_here):
            at = (block * heads_here + head) * nodes
            out_ref[block, head, 0] = summed[at : at + nodes]
            stats = jnp.where(lane == head, top[at : at + nodes], stats)
            stats = jnp.where(lane == heads_here + head, high[at : at + nodes], stats)
            stats = jnp.where(lane == 2 * heads_here + head, low[at : at + nodes], stats)
        out_ref[block, heads_here, 0] = stats.astype(jnp.bfloat16)


def attend(left, every_query, keys, values):
    column_count, requests, nodes, width_here = every_query.shape
    heads_here = width_here // HEAD_WIDTH
    kv_heads = keys.shape[2] // HEAD_WIDTH
    blocks = column_count // kv_heads
    prefix_here = keys.shape[1]
    return pl.pallas_call(
        functools.partial(attend_kernel, blocks * heads_here),
        grid_spec=pltpu.PrefetchScalarGridSpec(
            num_scalar_prefetch=1,
            grid=(requests, kv_heads),
            in_specs=[
                pl.BlockSpec((blocks, 1, nodes, width_here), lambda r, g, m: (g, r, 0, 0)),
                pl.BlockSpec((1, prefix_here, HEAD_WIDTH), lambda r, g, m: (r, 0, g)),
                pl.BlockSpec((1, prefix_here, HEAD_WIDTH), lambda r, g, m: (r, 0, g)),
            ],
            out_specs=pl.BlockSpec(
                (blocks, heads_here + 1, 1, nodes, HEAD_WIDTH), lambda r, g, m: (g, 0, r, 0, 0)
            ),
        ),
        out_shape=jax.ShapeDtypeStruct(
            (column_count, heads_here + 1, requests, nodes, HEAD_WIDTH), jnp.bfloat16
        ),
        compiler_params=params(),
        cost_estimate=pl.CostEstimate(
            flops=4 * requests * nodes * width_here * column_count * prefix_here,
            bytes_accessed=4 * requests * prefix_here * kv_heads * HEAD_WIDTH,
            transcendentals=requests * nodes * heads_here * column_count * prefix_here,
        ),
        name="attend",
    )(left, every_query, keys, values)


def merge_kernel(kv_ref, got_ref, q_ref, tk_ref, tv_ref, linked_ref, out_ref):
    sources, more, _, nodes, _ = got_ref.shape
    heads = more - 1
    query = jnp.concatenate(
        [q_ref[0, :, h * HEAD_WIDTH : (h + 1) * HEAD_WIDTH] for h in range(heads)], axis=0
    )
    linked = jnp.concatenate([linked_ref[0]] * heads, axis=0) > 0.5
    scores = dot(query, tk_ref[0], CONTRACT_LAST) * INV_ROOT
    top = jnp.max(jnp.where(linked, scores, NEG_FILL), axis=1, keepdims=True)
    tops, totals = [], []
    for source in range(sources):
        stats = got_ref[source, heads, 0].astype(jnp.float32)

        def columns(first):
            return jnp.concatenate([stats[:, first + h : first + h + 1] for h in range(heads)], axis=0)

        tops.append(columns(0))
        totals.append(columns(heads) + columns(2 * heads))
    for value in tops:
        top = jnp.maximum(top, value)
    weights = jnp.where(linked, jnp.exp(scores - top), 0.0)
    total = jnp.sum(weights, axis=1, keepdims=True)
    summed = dot(weights.astype(jnp.bfloat16), tv_ref[0])
    for source in range(sources):
        factor = jnp.exp(tops[source] - top)
        total = total + totals[source] * factor
        part = jnp.concatenate([got_ref[source, h, 0] for h in range(heads)], axis=0)
        summed = summed + part.astype(jnp.float32) * factor
    attended = (summed / total).astype(jnp.bfloat16)
    for h in range(heads):
        out_ref[0, :, h * HEAD_WIDTH : (h + 1) * HEAD_WIDTH] = attended[h * nodes : (h + 1) * nodes]


def merge(kv_group, got, queries, tree_keys, tree_values, linked):
    sources, more, requests, nodes, _ = got.shape
    width_here = queries.shape[2]
    return pl.pallas_call(
        merge_kernel,
        grid_spec=pltpu.PrefetchScalarGridSpec(
            num_scalar_prefetch=1,
            grid=(requests,),
            in_specs=[
                pl.BlockSpec((sources, more, 1, nodes, HEAD_WIDTH), lambda r, k: (0, 0, r, 0, 0)),
                pl.BlockSpec((1, nodes, width_here), lambda r, k: (r, 0, 0)),
                pl.BlockSpec((1, nodes, HEAD_WIDTH), lambda r, k: (r, 0, k[0])),
                pl.BlockSpec((1, nodes, HEAD_WIDTH), lambda r, k: (r, 0, k[0])),
                pl.BlockSpec((1, nodes, nodes), lambda r, k: (r, 0, 0)),
            ],
            out_specs=pl.BlockSpec((1, nodes, width_here), lambda r, k: (r, 0, 0)),
        ),
        out_shape=jax.ShapeDtypeStruct((requests, nodes, width_here), jnp.bfloat16),
        compiler_params=params(),
        name="merge",
    )(kv_group, got, queries, tree_keys, tree_values, linked)


def project_kernel(slot_ref, x_ref, down_ref, w_ref, out_ref, shrunk_ref):
    requests, nodes, width_here = x_ref.shape
    wide = w_ref.shape[1]

    @pl.when(pl.program_id(0) == 0)
    def _():
        shrunk_ref[...] = jnp.zeros_like(shrunk_ref)
        for r in range(requests):
            part = dot(x_ref[r], down_ref[slot_ref[r]], CONTRACT_LAST)
            shrunk_ref[r * nodes : (r + 1) * nodes, :ADAPTER_RANK] = part.astype(jnp.bfloat16)

    rows = x_ref[...].reshape(requests * nodes, width_here)
    out_ref[0, :, :wide] = dot(rows, w_ref[...]).astype(jnp.bfloat16)
    out_ref[0, :, wide:] = shrunk_ref[...]


def project(slot_code, attended, down, weight, columns):
    requests, nodes, width_here = attended.shape
    slots = down.shape[0]
    wide = weight.shape[1] // columns
    rows = requests * nodes
    return pl.pallas_call(
        project_kernel,
        grid_spec=pltpu.PrefetchScalarGridSpec(
            num_scalar_prefetch=1,
            grid=(columns,),
            in_specs=[
                pl.BlockSpec((requests, nodes, width_here), lambda c, s: (0, 0, 0)),
                pl.BlockSpec((slots, ADAPTER_RANK, width_here), lambda c, s: (0, 0, 0)),
                pl.BlockSpec((width_here, wide), lambda c, s: (0, c)),
            ],
            out_specs=pl.BlockSpec((1, rows, wide + LANES), lambda c, s: (c, 0, 0)),
            scratch_shapes=[pltpu.VMEM((rows, LANES), jnp.bfloat16)],
        ),
        out_shape=jax.ShapeDtypeStruct((columns, rows, wide + LANES), jnp.bfloat16),
        compiler_params=params(),
        name="project",
    )(slot_code, attended, down, weight)


def raise_kernel(slot_ref, base_ref, up_ref, out_ref):
    wide = out_ref.shape[2]
    shrunk = base_ref[:, wide : wide + ADAPTER_RANK]
    raised = dot(shrunk, up_ref[0])
    out_ref[0] = (base_ref[:, :wide].astype(jnp.float32) + ADAPTER_SCALE * raised).astype(
        jnp.bfloat16
    )


def finish(slot_code, base, up, requests):
    rows, wider = base.shape
    wide = wider - LANES
    nodes = rows // requests
    return pl.pallas_call(
        raise_kernel,
        grid_spec=pltpu.PrefetchScalarGridSpec(
            num_scalar_prefetch=1,
            grid=(requests,),
            in_specs=[
                pl.BlockSpec((nodes, wider), lambda r, s: (r, 0)),
                pl.BlockSpec((1, ADAPTER_RANK, wide), lambda r, s: (s[r], 0, 0)),
            ],
            out_specs=pl.BlockSpec((1, nodes, wide), lambda r, s: (r, 0, 0)),
        ),
        out_shape=jax.ShapeDtypeStruct((requests, nodes, wide), jnp.bfloat16),
        compiler_params=params(),
        name="finish",
    )(slot_code, base, up)


def per_device(
    queries,
    prefix_key_cache,
    prefix_value_cache,
    tree_node_keys,
    tree_node_values,
    lengths,
    parents,
    request_adapter_index,
    output_projection_weight,
    adapter_down_weight,
    adapter_up_weight,
):
    requests, nodes, width_here = queries.shape
    columns = lax.axis_size("mp")
    column = lax.axis_index("mp")
    heads_here = width_here // HEAD_WIDTH
    prefix_here = prefix_key_cache.shape[1]
    kv_heads = prefix_key_cache.shape[2] // HEAD_WIDTH
    group_size = heads_here * columns // kv_heads
    batch_size = lax.axis_size("batch")
    batch_row = lax.axis_index("batch")
    present, rank, _ = adapter_down_weight.shape

    every_ids = request_adapter_index.reshape(batch_size, requests)
    is_mine = every_ids // present == batch_row
    counted = is_mine.astype(jnp.int32)
    slot_rank = jnp.cumsum(counted, axis=1) - counted
    slot_ids = jnp.arange(CAP, dtype=jnp.int32)
    select = (slot_rank[:, None, :] == slot_ids[None, :, None]) & is_mine[:, None, :]
    picked = jnp.sum(jnp.where(select, (every_ids % present)[:, None, :], 0), axis=2).reshape(-1)
    send_down, send_up = pick(picked, adapter_down_weight, adapter_up_weight)
    down = lax.all_to_all(send_down, "batch", split_axis=0, concat_axis=0, tiled=True)
    up = lax.all_to_all(send_up, "batch", split_axis=0, concat_axis=0, tiled=True)
    mine_ids = lax.dynamic_slice_in_dim(request_adapter_index, batch_row * requests, requests)
    my_owner = mine_ids // present
    positions = jnp.arange(requests, dtype=jnp.int32)
    earlier = (my_owner[:, None] == my_owner[None, :]) & (positions[None, :] < positions[:, None])
    slot_code = my_owner * CAP + jnp.sum(earlier.astype(jnp.int32), axis=1)

    every_query = lax.all_gather(queries, "mp", axis=0)
    left = lengths - column * prefix_here
    partial = attend(left, every_query, prefix_key_cache, prefix_value_cache)
    got = lax.all_to_all(partial, "mp", split_axis=0, concat_axis=0, tiled=True)
    kv_group = (column * heads_here // group_size).reshape(1)
    attended = merge(
        kv_group, got, queries, tree_node_keys, tree_node_values, ancestors(parents)
    )
    shares = project(slot_code, attended, down, output_projection_weight, columns)
    base = lax.psum_scatter(shares, "mp", scatter_dimension=0, tiled=False)
    return finish(slot_code, base, up, requests)


def solution(mesh):
    return jax.shard_map(
        per_device,
        mesh=mesh,
        in_specs=(
            P(("groups", "batch"), None, "mp"),
            P(("groups", "batch"), "mp", None),
            P(("groups", "batch"), "mp", None),
            P(("groups", "batch"), None, None),
            P(("groups", "batch"), None, None),
            P(("groups", "batch")),
            P(("groups", "batch"), None),
            P("groups"),
            P("mp", None),
            P("batch", None, "mp"),
            P("batch", None, "mp"),
        ),
        out_specs=P(("groups", "batch"), None, "mp"),
        check_vma=False,
    )
```

```python
import functools
import math

import jax
import jax.numpy as jnp
from jax import lax
from jax.experimental import pallas as pl
from jax.experimental.pallas import tpu as pltpu
from jax.sharding import PartitionSpec as P

HEAD_WIDTH = 128
ADAPTER_RANK = 64
CAP = 2
LANES = 128
NEG_FILL = -1e30
ADAPTER_SCALE = 2.0
INV_ROOT = 1.0 / math.sqrt(HEAD_WIDTH)
VMEM_LIMIT = 48 << 20
CONTRACT_LAST = (((1,), (1,)), ((), ()))
CONTRACT_INNER = (((1,), (0,)), ((), ()))


def dot(a, b, dims=CONTRACT_INNER):
    return lax.dot_general(a, b, dims, preferred_element_type=jnp.float32)


def params(**more):
    return pltpu.CompilerParams(vmem_limit_bytes=VMEM_LIMIT, **more)


def ancestors(parents):
    tree_node_count = parents.shape[-1]
    identity_mat = jnp.eye(tree_node_count, dtype=jnp.float32)
    parent_mat = (
        parents[..., :, None] == jnp.arange(tree_node_count, dtype=jnp.int32)[None, :]
    ).astype(jnp.float32)
    reached = jnp.minimum(identity_mat + parent_mat, 1.0)
    for repeat in range(max(1, (tree_node_count - 1).bit_length())):
        step = reached.astype(jnp.bfloat16)
        reached = jnp.minimum(
            jnp.einsum("rnm,rmk->rnk", step, step, preferred_element_type=jnp.float32), 1.0
        )
    return reached


def pick_kernel(shifts, picked_ref, left_ref, down_ref, up_ref, left_out, *rest):
    firsts, seconds, sems = rest[:shifts], rest[shifts : 2 * shifts], rest[2 * shifts]
    half = up_ref.shape[2] // 2
    width = down_ref.shape[2]
    copies = []
    for shift in range(shifts):
        for slot in range(CAP):
            at = shift * CAP + slot
            index = picked_ref[at]
            pairs = (
                (up_ref.at[index, :, pl.ds(0, half)], firsts[shift].at[slot, :, pl.ds(0, half)]),
                (down_ref.at[index], firsts[shift].at[slot, :, pl.ds(half, width)]),
                (up_ref.at[index, :, pl.ds(half, half)], seconds[shift].at[slot]),
            )
            for which, (source, target) in enumerate(pairs):
                copies.append(pltpu.make_async_copy(source, target, sems.at[which, at]))
    for copy in copies:
        copy.start()
    for r in range(left_ref.shape[0]):
        left_out[r] = left_ref[r]
    for copy in copies:
        copy.wait()


def pick(picked, left, down, up):
    shifts = picked.shape[0] // CAP
    hbm = pl.BlockSpec(memory_space=pl.ANY)
    smem = pl.BlockSpec(memory_space=pltpu.SMEM)
    half = up.shape[2] // 2
    first = jax.ShapeDtypeStruct((CAP, up.shape[1], half + down.shape[2]), up.dtype)
    second = jax.ShapeDtypeStruct((CAP, up.shape[1], half), up.dtype)
    out = pl.pallas_call(
        functools.partial(pick_kernel, shifts),
        in_specs=[smem, smem, hbm, hbm],
        out_specs=[smem] + [hbm] * (2 * shifts),
        out_shape=[jax.ShapeDtypeStruct(left.shape, left.dtype)]
        + [first] * shifts
        + [second] * shifts,
        scratch_shapes=[pltpu.SemaphoreType.DMA((3, shifts * CAP))],
        compiler_params=params(),
        name="pick",
    )(picked, left, down, up)
    return out[0], out[1 : 1 + shifts], out[1 + shifts :]


def exchange(blocks, axis):
    size = len(blocks)
    got = [blocks[0]]
    for shift in range(1, size):
        pairs = [(i, (i + shift) % size) for i in range(size)]
        got.append(lax.ppermute(blocks[shift], axis, pairs))
    return got


def attend_kernel(blocks, meta_ref, *refs):
    q_refs = refs[:blocks]
    k_ref, v_ref, out_ref = refs[blocks:]
    _, _, nodes, width_here = q_refs[0].shape
    heads_here = width_here // HEAD_WIDTH
    request = pl.program_id(0)
    positions = k_ref.shape[1]
    left = meta_ref[request]
    rows = []
    for block in range(blocks):
        for head in range(heads_here):
            rows.append(q_refs[block][0, 0, :, head * HEAD_WIDTH : (head + 1) * HEAD_WIDTH])
    query = jnp.concatenate(rows, axis=0)
    scores = dot(query, k_ref[0], CONTRACT_LAST) * INV_ROOT
    place = lax.broadcasted_iota(jnp.int32, (1, positions), 1)
    valid = place < left
    scores = jnp.where(valid, scores, NEG_FILL)
    top = jnp.max(scores, axis=1, keepdims=True).astype(jnp.bfloat16).astype(jnp.float32)
    weights = jnp.where(valid, jnp.exp(scores - top), 0.0)
    total = jnp.sum(weights, axis=1, keepdims=True)
    summed = dot(weights.astype(jnp.bfloat16), v_ref[0]).astype(jnp.bfloat16)
    high = total.astype(jnp.bfloat16).astype(jnp.float32)
    low = total - high
    lane = lax.broadcasted_iota(jnp.int32, (nodes, LANES), 1)
    for block in range(blocks):
        stats = jnp.zeros((nodes, LANES), jnp.float32)
        for head in range(heads_here):
            at = (block * heads_here + head) * nodes
            out_ref[block, head, 0] = summed[at : at + nodes]
            stats = jnp.where(lane == head, top[at : at + nodes], stats)
            stats = jnp.where(lane == heads_here + head, high[at : at + nodes], stats)
            stats = jnp.where(lane == 2 * heads_here + head, low[at : at + nodes], stats)
        out_ref[block, heads_here, 0] = stats.astype(jnp.bfloat16)


def attend(meta, every_query, keys, values):
    column_count, requests, nodes, width_here = every_query.shape
    heads_here = width_here // HEAD_WIDTH
    kv_heads = keys.shape[2] // HEAD_WIDTH
    blocks = column_count // kv_heads
    prefix_here = keys.shape[1]

    def query_spec(block):
        def index(r, g, m):
            return (m[requests] - (g * blocks + block) + column_count) % column_count, r, 0, 0

        return pl.BlockSpec((1, 1, nodes, width_here), index)

    return pl.pallas_call(
        functools.partial(attend_kernel, blocks),
        grid_spec=pltpu.PrefetchScalarGridSpec(
            num_scalar_prefetch=1,
            grid=(requests, kv_heads),
            in_specs=[
                *[query_spec(block) for block in range(blocks)],
                pl.BlockSpec((1, prefix_here, HEAD_WIDTH), lambda r, g, m: (r, 0, g)),
                pl.BlockSpec((1, prefix_here, HEAD_WIDTH), lambda r, g, m: (r, 0, g)),
            ],
            out_specs=pl.BlockSpec(
                (blocks, heads_here + 1, 1, nodes, HEAD_WIDTH), lambda r, g, m: (g, 0, r, 0, 0)
            ),
        ),
        out_shape=jax.ShapeDtypeStruct(
            (column_count, heads_here + 1, requests, nodes, HEAD_WIDTH), jnp.bfloat16
        ),
        compiler_params=params(),
        cost_estimate=pl.CostEstimate(
            flops=4 * requests * nodes * width_here * column_count * prefix_here,
            bytes_accessed=4 * requests * prefix_here * kv_heads * HEAD_WIDTH,
            transcendentals=requests * nodes * heads_here * column_count * prefix_here,
        ),
        name="attend",
    )(meta, *[every_query] * blocks, keys, values)


def merge_kernel(kv_ref, got_ref, q_ref, tk_ref, tv_ref, linked_ref, out_ref):
    sources, more, _, nodes, _ = got_ref.shape
    heads = more - 1
    query = jnp.concatenate(
        [q_ref[0, :, h * HEAD_WIDTH : (h + 1) * HEAD_WIDTH] for h in range(heads)], axis=0
    )
    linked = jnp.concatenate([linked_ref[0]] * heads, axis=0) > 0.5
    scores = dot(query, tk_ref[0], CONTRACT_LAST) * INV_ROOT
    top = jnp.max(jnp.where(linked, scores, NEG_FILL), axis=1, keepdims=True)
    tops, totals = [], []
    for source in range(sources):
        stats = got_ref[source, heads, 0].astype(jnp.float32)

        def columns(first):
            return jnp.concatenate([stats[:, first + h : first + h + 1] for h in range(heads)], axis=0)

        tops.append(columns(0))
        totals.append(columns(heads) + columns(2 * heads))
    for value in tops:
        top = jnp.maximum(top, value)
    weights = jnp.where(linked, jnp.exp(scores - top), 0.0)
    total = jnp.sum(weights, axis=1, keepdims=True)
    summed = dot(weights.astype(jnp.bfloat16), tv_ref[0])
    for source in range(sources):
        factor = jnp.exp(tops[source] - top)
        total = total + totals[source] * factor
        part = jnp.concatenate([got_ref[source, h, 0] for h in range(heads)], axis=0)
        summed = summed + part.astype(jnp.float32) * factor
    attended = (summed / total).astype(jnp.bfloat16)
    for h in range(heads):
        out_ref[0, :, h * HEAD_WIDTH : (h + 1) * HEAD_WIDTH] = attended[h * nodes : (h + 1) * nodes]


def merge(kv_group, got, queries, tree_keys, tree_values, linked):
    sources, more, requests, nodes, _ = got.shape
    width_here = queries.shape[2]
    return pl.pallas_call(
        merge_kernel,
        grid_spec=pltpu.PrefetchScalarGridSpec(
            num_scalar_prefetch=1,
            grid=(requests,),
            in_specs=[
                pl.BlockSpec((sources, more, 1, nodes, HEAD_WIDTH), lambda r, k: (0, 0, r, 0, 0)),
                pl.BlockSpec((1, nodes, width_here), lambda r, k: (r, 0, 0)),
                pl.BlockSpec((1, nodes, HEAD_WIDTH), lambda r, k: (r, 0, k[0])),
                pl.BlockSpec((1, nodes, HEAD_WIDTH), lambda r, k: (r, 0, k[0])),
                pl.BlockSpec((1, nodes, nodes), lambda r, k: (r, 0, 0)),
            ],
            out_specs=pl.BlockSpec((1, nodes, width_here), lambda r, k: (r, 0, 0)),
        ),
        out_shape=jax.ShapeDtypeStruct((requests, nodes, width_here), jnp.bfloat16),
        compiler_params=params(),
        name="merge",
    )(kv_group, got, queries, tree_keys, tree_values, linked)


def project_kernel(slot_ref, x_ref, down_ref, w_ref, out_ref, shrunk_ref):
    requests, nodes, width_here = x_ref.shape
    wide = w_ref.shape[1]

    @pl.when(pl.program_id(0) == 0)
    def _():
        shrunk_ref[...] = jnp.zeros_like(shrunk_ref)
        for r in range(requests):
            part = dot(x_ref[r], down_ref[slot_ref[r]], CONTRACT_LAST)
            shrunk_ref[r * nodes : (r + 1) * nodes, :ADAPTER_RANK] = part.astype(jnp.bfloat16)

    rows = x_ref[...].reshape(requests * nodes, width_here)
    out_ref[0, :, :wide] = dot(rows, w_ref[...]).astype(jnp.bfloat16)
    out_ref[0, :, wide:] = shrunk_ref[...]


def project(slot_code, attended, maps, weight, columns):
    requests, nodes, width_here = attended.shape
    slots = maps.shape[0]
    down_block = maps.shape[2] // width_here - 1
    wide = weight.shape[1] // columns
    rows = requests * nodes
    return pl.pallas_call(
        project_kernel,
        grid_spec=pltpu.PrefetchScalarGridSpec(
            num_scalar_prefetch=1,
            grid=(columns,),
            in_specs=[
                pl.BlockSpec((requests, nodes, width_here), lambda c, s: (0, 0, 0)),
                pl.BlockSpec((slots, ADAPTER_RANK, width_here), lambda c, s: (0, 0, down_block)),
                pl.BlockSpec((width_here, wide), lambda c, s: (0, c)),
            ],
            out_specs=pl.BlockSpec((1, rows, wide + LANES), lambda c, s: (c, 0, 0)),
            scratch_shapes=[pltpu.VMEM((rows, LANES), jnp.bfloat16)],
        ),
        out_shape=jax.ShapeDtypeStruct((columns, rows, wide + LANES), jnp.bfloat16),
        compiler_params=params(),
        name="project",
    )(slot_code, attended, maps, weight)


def raise_kernel(slot_ref, base_ref, first_ref, second_ref, out_ref):
    wide = out_ref.shape[2]
    half = wide // 2
    shrunk = base_ref[:, wide : wide + ADAPTER_RANK]
    for at, up_ref in ((0, first_ref), (half, second_ref)):
        raised = dot(shrunk, up_ref[0])
        projected = base_ref[:, at : at + half].astype(jnp.float32)
        out_ref[0, :, at : at + half] = (projected + ADAPTER_SCALE * raised).astype(jnp.bfloat16)


def finish(slot_code, base, maps, rest, requests):
    rows, wider = base.shape
    wide = wider - LANES
    nodes = rows // requests
    up_spec = pl.BlockSpec((1, ADAPTER_RANK, wide // 2), lambda r, s: (s[r], 0, 0))
    return pl.pallas_call(
        raise_kernel,
        grid_spec=pltpu.PrefetchScalarGridSpec(
            num_scalar_prefetch=1,
            grid=(requests,),
            in_specs=[pl.BlockSpec((nodes, wider), lambda r, s: (r, 0)), up_spec, up_spec],
            out_specs=pl.BlockSpec((1, nodes, wide), lambda r, s: (r, 0, 0)),
        ),
        out_shape=jax.ShapeDtypeStruct((requests, nodes, wide), jnp.bfloat16),
        compiler_params=params(),
        name="finish",
    )(slot_code, base, maps, rest)


def per_device(
    queries,
    prefix_key_cache,
    prefix_value_cache,
    tree_node_keys,
    tree_node_values,
    lengths,
    parents,
    request_adapter_index,
    output_projection_weight,
    adapter_down_weight,
    adapter_up_weight,
):
    requests, nodes, width_here = queries.shape
    columns = lax.axis_size("mp")
    column = lax.axis_index("mp")
    heads_here = width_here // HEAD_WIDTH
    prefix_here = prefix_key_cache.shape[1]
    kv_heads = prefix_key_cache.shape[2] // HEAD_WIDTH
    group_size = heads_here * columns // kv_heads
    batch_size = lax.axis_size("batch")
    batch_row = lax.axis_index("batch")
    present, rank, _ = adapter_down_weight.shape

    every_ids = request_adapter_index.reshape(batch_size, requests)
    is_mine = every_ids // present == batch_row
    counted = is_mine.astype(jnp.int32)
    slot_rank = jnp.cumsum(counted, axis=1) - counted
    slot_ids = jnp.arange(CAP, dtype=jnp.int32)
    select = (slot_rank[:, None, :] == slot_ids[None, :, None]) & is_mine[:, None, :]
    picked = jnp.sum(jnp.where(select, (every_ids % present)[:, None, :], 0), axis=2)
    target = (batch_row + jnp.arange(batch_size, dtype=jnp.int32)) % batch_size
    chosen = target[:, None] == jnp.arange(batch_size, dtype=jnp.int32)[None, :]
    picked = jnp.sum(jnp.where(chosen[:, :, None], picked[None], 0), axis=1).reshape(-1)
    left, firsts, seconds = pick(
        picked, lengths - column * prefix_here, adapter_down_weight, adapter_up_weight
    )
    maps = jnp.concatenate(exchange(firsts, "batch"), axis=0)
    rest = jnp.concatenate(exchange(seconds, "batch"), axis=0)
    mine_ids = lax.dynamic_slice_in_dim(request_adapter_index, batch_row * requests, requests)
    my_owner = mine_ids // present
    positions = jnp.arange(requests, dtype=jnp.int32)
    earlier = (my_owner[:, None] == my_owner[None, :]) & (positions[None, :] < positions[:, None])
    distance = (batch_row - my_owner + batch_size) % batch_size
    slot_code = distance * CAP + jnp.sum(earlier.astype(jnp.int32), axis=1)

    every_query = jnp.stack(exchange([queries] * columns, "mp"), axis=0)
    meta = jnp.concatenate([left, column.reshape(1)])
    partial = attend(meta, every_query, prefix_key_cache, prefix_value_cache)
    got = lax.all_to_all(partial, "mp", split_axis=0, concat_axis=0, tiled=True)
    kv_group = (column * heads_here // group_size).reshape(1)
    attended = merge(
        kv_group, got, queries, tree_node_keys, tree_node_values, ancestors(parents)
    )
    shares = project(slot_code, attended, maps, output_projection_weight, columns)
    base = lax.psum_scatter(shares, "mp", scatter_dimension=0, tiled=False)
    return finish(slot_code, base, maps, rest, requests)


def solution(mesh):
    return jax.shard_map(
        per_device,
        mesh=mesh,
        in_specs=(
            P(("groups", "batch"), None, "mp"),
            P(("groups", "batch"), "mp", None),
            P(("groups", "batch"), "mp", None),
            P(("groups", "batch"), None, None),
            P(("groups", "batch"), None, None),
            P(("groups", "batch")),
            P(("groups", "batch"), None),
            P("groups"),
            P("mp", None),
            P("batch", None, "mp"),
            P("batch", None, "mp"),
        ),
        out_specs=P(("groups", "batch"), None, "mp"),
        check_vma=False,
    )
```

```python
import functools
import math

import jax
import jax.numpy as jnp
from jax import lax
from jax.experimental import pallas as pl
from jax.experimental.pallas import tpu as pltpu
from jax.sharding import PartitionSpec as P

HEAD_WIDTH = 128
ADAPTER_RANK = 64
CAP = 2
LANES = 128
NEG_FILL = -1e30
ADAPTER_SCALE = 2.0
INV_ROOT = 1.0 / math.sqrt(HEAD_WIDTH)
VMEM_LIMIT = 48 << 20
CONTRACT_LAST = (((1,), (1,)), ((), ()))
CONTRACT_INNER = (((1,), (0,)), ((), ()))


def dot(a, b, dims=CONTRACT_INNER):
    return lax.dot_general(a, b, dims, preferred_element_type=jnp.float32)


def params(**more):
    return pltpu.CompilerParams(vmem_limit_bytes=VMEM_LIMIT, **more)


def ancestors(parents):
    tree_node_count = parents.shape[-1]
    identity_mat = jnp.eye(tree_node_count, dtype=jnp.float32)
    parent_mat = (
        parents[..., :, None] == jnp.arange(tree_node_count, dtype=jnp.int32)[None, :]
    ).astype(jnp.float32)
    reached = jnp.minimum(identity_mat + parent_mat, 1.0)
    for repeat in range(max(1, (tree_node_count - 1).bit_length())):
        step = reached.astype(jnp.bfloat16)
        reached = jnp.minimum(
            jnp.einsum("rnm,rmk->rnk", step, step, preferred_element_type=jnp.float32), 1.0
        )
    return reached


def pick_kernel(shifts, picked_ref, left_ref, down_ref, up_ref, left_out, *rest):
    firsts, seconds, sems = rest[:shifts], rest[shifts : 2 * shifts], rest[2 * shifts]
    half = up_ref.shape[2] // 2
    width = down_ref.shape[2]
    copies = []
    for shift in range(shifts):
        for slot in range(CAP):
            at = shift * CAP + slot
            index = picked_ref[at]
            pairs = (
                (up_ref.at[index, :, pl.ds(0, half)], firsts[shift].at[slot, :, pl.ds(0, half)]),
                (down_ref.at[index], firsts[shift].at[slot, :, pl.ds(half, width)]),
                (up_ref.at[index, :, pl.ds(half, half)], seconds[shift].at[slot]),
            )
            for which, (source, target) in enumerate(pairs):
                copies.append(pltpu.make_async_copy(source, target, sems.at[which, at]))
    for copy in copies:
        copy.start()
    for r in range(left_ref.shape[0]):
        left_out[r] = left_ref[r]
    for copy in copies:
        copy.wait()


def pick(picked, left, down, up):
    shifts = picked.shape[0] // CAP
    hbm = pl.BlockSpec(memory_space=pl.ANY)
    smem = pl.BlockSpec(memory_space=pltpu.SMEM)
    half = up.shape[2] // 2
    first = jax.ShapeDtypeStruct((CAP, up.shape[1], half + down.shape[2]), up.dtype)
    second = jax.ShapeDtypeStruct((CAP, up.shape[1], half), up.dtype)
    out = pl.pallas_call(
        functools.partial(pick_kernel, shifts),
        in_specs=[smem, smem, hbm, hbm],
        out_specs=[smem] + [hbm] * (2 * shifts),
        out_shape=[jax.ShapeDtypeStruct(left.shape, left.dtype)]
        + [first] * shifts
        + [second] * shifts,
        scratch_shapes=[pltpu.SemaphoreType.DMA((3, shifts * CAP))],
        compiler_params=params(),
        name="pick",
    )(picked, left, down, up)
    return out[0], out[1 : 1 + shifts], out[1 + shifts :]


def exchange(blocks, axis):
    size = len(blocks)
    got = [blocks[0]]
    for shift in range(1, size):
        pairs = [(i, (i + shift) % size) for i in range(size)]
        got.append(lax.ppermute(blocks[shift], axis, pairs))
    return got


def attend_kernel(blocks, meta_ref, *refs):
    q_refs = refs[:blocks]
    k_ref, v_ref, out_ref = refs[blocks:]
    _, _, nodes, width_here = q_refs[0].shape
    heads_here = width_here // HEAD_WIDTH
    request = pl.program_id(0)
    positions = k_ref.shape[1]
    left = meta_ref[request]
    rows = []
    for block in range(blocks):
        for head in range(heads_here):
            rows.append(q_refs[block][0, 0, :, head * HEAD_WIDTH : (head + 1) * HEAD_WIDTH])
    query = jnp.concatenate(rows, axis=0)
    scores = dot(query, k_ref[0], CONTRACT_LAST) * INV_ROOT
    place = lax.broadcasted_iota(jnp.int32, (1, positions), 1)
    valid = place < left
    scores = jnp.where(valid, scores, NEG_FILL)
    top = jnp.max(scores, axis=1, keepdims=True).astype(jnp.bfloat16).astype(jnp.float32)
    weights = jnp.where(valid, jnp.exp(scores - top), 0.0)
    total = jnp.sum(weights, axis=1, keepdims=True)
    summed = dot(weights.astype(jnp.bfloat16), v_ref[0]).astype(jnp.bfloat16)
    high = total.astype(jnp.bfloat16).astype(jnp.float32)
    low = total - high
    lane = lax.broadcasted_iota(jnp.int32, (nodes, LANES), 1)
    for block in range(blocks):
        stats = jnp.zeros((nodes, LANES), jnp.float32)
        for head in range(heads_here):
            at = (block * heads_here + head) * nodes
            out_ref[block, head, 0] = summed[at : at + nodes]
            stats = jnp.where(lane == head, top[at : at + nodes], stats)
            stats = jnp.where(lane == heads_here + head, high[at : at + nodes], stats)
            stats = jnp.where(lane == 2 * heads_here + head, low[at : at + nodes], stats)
        out_ref[block, heads_here, 0] = stats.astype(jnp.bfloat16)


def attend(meta, every_query, keys, values):
    column_count, requests, nodes, width_here = every_query.shape
    heads_here = width_here // HEAD_WIDTH
    kv_heads = keys.shape[2] // HEAD_WIDTH
    blocks = column_count // kv_heads
    prefix_here = keys.shape[1]

    def query_spec(block):
        def index(r, g, m):
            return (m[requests] - (g * blocks + block) + column_count) % column_count, r, 0, 0

        return pl.BlockSpec((1, 1, nodes, width_here), index)

    return pl.pallas_call(
        functools.partial(attend_kernel, blocks),
        grid_spec=pltpu.PrefetchScalarGridSpec(
            num_scalar_prefetch=1,
            grid=(requests, kv_heads),
            in_specs=[
                *[query_spec(block) for block in range(blocks)],
                pl.BlockSpec((1, prefix_here, HEAD_WIDTH), lambda r, g, m: (r, 0, g)),
                pl.BlockSpec((1, prefix_here, HEAD_WIDTH), lambda r, g, m: (r, 0, g)),
            ],
            out_specs=pl.BlockSpec(
                (blocks, heads_here + 1, 1, nodes, HEAD_WIDTH), lambda r, g, m: (g, 0, r, 0, 0)
            ),
        ),
        out_shape=jax.ShapeDtypeStruct(
            (column_count, heads_here + 1, requests, nodes, HEAD_WIDTH), jnp.bfloat16
        ),
        compiler_params=params(),
        cost_estimate=pl.CostEstimate(
            flops=4 * requests * nodes * width_here * column_count * prefix_here,
            bytes_accessed=4 * requests * prefix_here * kv_heads * HEAD_WIDTH,
            transcendentals=requests * nodes * heads_here * column_count * prefix_here,
        ),
        name="attend",
    )(meta, *[every_query] * blocks, keys, values)


def merge_kernel(kv_ref, got_ref, q_ref, tk_ref, tv_ref, linked_ref, out_ref):
    sources, more, _, nodes, _ = got_ref.shape
    heads = more - 1
    query = jnp.concatenate(
        [q_ref[0, :, h * HEAD_WIDTH : (h + 1) * HEAD_WIDTH] for h in range(heads)], axis=0
    )
    linked = jnp.concatenate([linked_ref[0]] * heads, axis=0) > 0.5
    scores = dot(query, tk_ref[0], CONTRACT_LAST) * INV_ROOT
    top = jnp.max(jnp.where(linked, scores, NEG_FILL), axis=1, keepdims=True)
    tops, totals = [], []
    for source in range(sources):
        stats = got_ref[source, heads, 0].astype(jnp.float32)

        def columns(first):
            return jnp.concatenate([stats[:, first + h : first + h + 1] for h in range(heads)], axis=0)

        tops.append(columns(0))
        totals.append(columns(heads) + columns(2 * heads))
    for value in tops:
        top = jnp.maximum(top, value)
    weights = jnp.where(linked, jnp.exp(scores - top), 0.0)
    total = jnp.sum(weights, axis=1, keepdims=True)
    summed = dot(weights.astype(jnp.bfloat16), tv_ref[0])
    for source in range(sources):
        factor = jnp.exp(tops[source] - top)
        total = total + totals[source] * factor
        part = jnp.concatenate([got_ref[source, h, 0] for h in range(heads)], axis=0)
        summed = summed + part.astype(jnp.float32) * factor
    attended = (summed / total).astype(jnp.bfloat16)
    for h in range(heads):
        out_ref[0, :, h * HEAD_WIDTH : (h + 1) * HEAD_WIDTH] = attended[h * nodes : (h + 1) * nodes]


def merge(kv_group, got, queries, tree_keys, tree_values, linked):
    sources, more, requests, nodes, _ = got.shape
    width_here = queries.shape[2]
    return pl.pallas_call(
        merge_kernel,
        grid_spec=pltpu.PrefetchScalarGridSpec(
            num_scalar_prefetch=1,
            grid=(requests,),
            in_specs=[
                pl.BlockSpec((sources, more, 1, nodes, HEAD_WIDTH), lambda r, k: (0, 0, r, 0, 0)),
                pl.BlockSpec((1, nodes, width_here), lambda r, k: (r, 0, 0)),
                pl.BlockSpec((1, nodes, HEAD_WIDTH), lambda r, k: (r, 0, k[0])),
                pl.BlockSpec((1, nodes, HEAD_WIDTH), lambda r, k: (r, 0, k[0])),
                pl.BlockSpec((1, nodes, nodes), lambda r, k: (r, 0, 0)),
            ],
            out_specs=pl.BlockSpec((1, nodes, width_here), lambda r, k: (r, 0, 0)),
        ),
        out_shape=jax.ShapeDtypeStruct((requests, nodes, width_here), jnp.bfloat16),
        compiler_params=params(),
        name="merge",
    )(kv_group, got, queries, tree_keys, tree_values, linked)


def project_kernel(slot_ref, x_ref, down_ref, w_ref, out_ref):
    requests, nodes, width_here = x_ref.shape
    wide = w_ref.shape[1]
    rows = x_ref[...].reshape(requests * nodes, width_here)
    out_ref[:, :wide] = dot(rows, w_ref[...]).astype(jnp.bfloat16)
    out_ref[:, wide:] = jnp.zeros((requests * nodes, LANES), jnp.bfloat16)
    for r in range(requests):
        part = dot(x_ref[r], down_ref[slot_ref[r]], CONTRACT_LAST)
        out_ref[r * nodes : (r + 1) * nodes, wide : wide + ADAPTER_RANK] = part.astype(jnp.bfloat16)


def project(meta, attended, maps, weight, columns):
    requests, nodes, width_here = attended.shape
    slots = maps.shape[0]
    down_block = maps.shape[2] // width_here - 1
    wide = weight.shape[1] // columns
    rows = requests * nodes
    return pl.pallas_call(
        project_kernel,
        grid_spec=pltpu.PrefetchScalarGridSpec(
            num_scalar_prefetch=1,
            grid=(1,),
            in_specs=[
                pl.BlockSpec((requests, nodes, width_here), lambda i, s: (0, 0, 0)),
                pl.BlockSpec((slots, ADAPTER_RANK, width_here), lambda i, s: (0, 0, down_block)),
                pl.BlockSpec((width_here, wide), lambda i, s: (0, s[requests])),
            ],
            out_specs=pl.BlockSpec((rows, wide + LANES), lambda i, s: (0, 0)),
        ),
        out_shape=jax.ShapeDtypeStruct((rows, wide + LANES), jnp.bfloat16),
        compiler_params=params(),
        cost_estimate=pl.CostEstimate(
            flops=2 * rows * width_here * wide,
            bytes_accessed=2 * width_here * wide,
            transcendentals=0,
        ),
        name="project",
    )(meta, attended, maps, weight)


def raise_kernel(slot_ref, first_ref, second_ref, *refs):
    share_refs, out_ref = refs[:-1], refs[-1]
    wide = out_ref.shape[2]
    half = wide // 2

    def added(start, size):
        total = share_refs[0][:, start : start + size].astype(jnp.float32)
        for share_ref in share_refs[1:]:
            total = total + share_ref[:, start : start + size].astype(jnp.float32)
        return total

    shrunk = added(wide, LANES)[:, :ADAPTER_RANK].astype(jnp.bfloat16)
    for at, up_ref in ((0, first_ref), (half, second_ref)):
        raised = dot(shrunk, up_ref[0])
        out_ref[0, :, at : at + half] = (added(at, half) + ADAPTER_SCALE * raised).astype(
            jnp.bfloat16
        )


def finish(slot_code, shares, maps, rest, requests):
    rows, wider = shares[0].shape
    wide = wider - LANES
    nodes = rows // requests
    up_spec = pl.BlockSpec((1, ADAPTER_RANK, wide // 2), lambda r, s: (s[r], 0, 0))
    share_spec = pl.BlockSpec((nodes, wider), lambda r, s: (r, 0))
    return pl.pallas_call(
        raise_kernel,
        grid_spec=pltpu.PrefetchScalarGridSpec(
            num_scalar_prefetch=1,
            grid=(requests,),
            in_specs=[up_spec, up_spec] + [share_spec] * len(shares),
            out_specs=pl.BlockSpec((1, nodes, wide), lambda r, s: (r, 0, 0)),
        ),
        out_shape=jax.ShapeDtypeStruct((requests, nodes, wide), jnp.bfloat16),
        compiler_params=params(),
        name="finish",
    )(slot_code, maps, rest, *shares)


def per_device(
    queries,
    prefix_key_cache,
    prefix_value_cache,
    tree_node_keys,
    tree_node_values,
    lengths,
    parents,
    request_adapter_index,
    output_projection_weight,
    adapter_down_weight,
    adapter_up_weight,
):
    requests, nodes, width_here = queries.shape
    columns = lax.axis_size("mp")
    column = lax.axis_index("mp")
    heads_here = width_here // HEAD_WIDTH
    prefix_here = prefix_key_cache.shape[1]
    kv_heads = prefix_key_cache.shape[2] // HEAD_WIDTH
    group_size = heads_here * columns // kv_heads
    batch_size = lax.axis_size("batch")
    batch_row = lax.axis_index("batch")
    present, rank, _ = adapter_down_weight.shape

    every_ids = request_adapter_index.reshape(batch_size, requests)
    is_mine = every_ids // present == batch_row
    counted = is_mine.astype(jnp.int32)
    slot_rank = jnp.cumsum(counted, axis=1) - counted
    slot_ids = jnp.arange(CAP, dtype=jnp.int32)
    select = (slot_rank[:, None, :] == slot_ids[None, :, None]) & is_mine[:, None, :]
    picked = jnp.sum(jnp.where(select, (every_ids % present)[:, None, :], 0), axis=2)
    target = (batch_row + jnp.arange(batch_size, dtype=jnp.int32)) % batch_size
    chosen = target[:, None] == jnp.arange(batch_size, dtype=jnp.int32)[None, :]
    picked = jnp.sum(jnp.where(chosen[:, :, None], picked[None], 0), axis=1).reshape(-1)
    left, firsts, seconds = pick(
        picked, lengths - column * prefix_here, adapter_down_weight, adapter_up_weight
    )
    maps = jnp.concatenate(exchange(firsts, "batch"), axis=0)
    rest = jnp.concatenate(exchange(seconds, "batch"), axis=0)
    mine_ids = lax.dynamic_slice_in_dim(request_adapter_index, batch_row * requests, requests)
    my_owner = mine_ids // present
    positions = jnp.arange(requests, dtype=jnp.int32)
    earlier = (my_owner[:, None] == my_owner[None, :]) & (positions[None, :] < positions[:, None])
    distance = (batch_row - my_owner + batch_size) % batch_size
    slot_code = distance * CAP + jnp.sum(earlier.astype(jnp.int32), axis=1)

    every_query = jnp.stack(exchange([queries] * columns, "mp"), axis=0)
    meta = jnp.concatenate([left, column.reshape(1)])
    partial = attend(meta, every_query, prefix_key_cache, prefix_value_cache)
    got = lax.all_to_all(partial, "mp", split_axis=0, concat_axis=0, tiled=True)
    kv_group = (column * heads_here // group_size).reshape(1)
    attended = merge(
        kv_group, got, queries, tree_node_keys, tree_node_values, ancestors(parents)
    )
    shares = []
    for shift in range(columns):
        target_column = ((column + shift) % columns).reshape(1)
        project_meta = jnp.concatenate([slot_code, target_column])
        shares.append(project(project_meta, attended, maps, output_projection_weight, columns))
    return finish(slot_code, exchange(shares, "mp"), maps, rest, requests)


def solution(mesh):
    return jax.shard_map(
        per_device,
        mesh=mesh,
        in_specs=(
            P(("groups", "batch"), None, "mp"),
            P(("groups", "batch"), "mp", None),
            P(("groups", "batch"), "mp", None),
            P(("groups", "batch"), None, None),
            P(("groups", "batch"), None, None),
            P(("groups", "batch")),
            P(("groups", "batch"), None),
            P("groups"),
            P("mp", None),
            P("batch", None, "mp"),
            P("batch", None, "mp"),
        ),
        out_specs=P(("groups", "batch"), None, "mp"),
        check_vma=False,
    )
```

```python
import functools
import math

import jax
import jax.numpy as jnp
from jax import lax
from jax.experimental import pallas as pl
from jax.experimental.pallas import tpu as pltpu
from jax.sharding import PartitionSpec as P

HEAD_WIDTH = 128
ADAPTER_RANK = 64
CAP = 2
LANES = 128
NEG_FILL = -1e30
ADAPTER_SCALE = 2.0
INV_ROOT = 1.0 / math.sqrt(HEAD_WIDTH)
VMEM_LIMIT = 48 << 20
CONTRACT_LAST = (((1,), (1,)), ((), ()))
CONTRACT_INNER = (((1,), (0,)), ((), ()))


def dot(a, b, dims=CONTRACT_INNER):
    return lax.dot_general(a, b, dims, preferred_element_type=jnp.float32)


def params(**more):
    return pltpu.CompilerParams(vmem_limit_bytes=VMEM_LIMIT, **more)


def ancestors(parents):
    tree_node_count = parents.shape[-1]
    identity_mat = jnp.eye(tree_node_count, dtype=jnp.float32)
    parent_mat = (
        parents[..., :, None] == jnp.arange(tree_node_count, dtype=jnp.int32)[None, :]
    ).astype(jnp.float32)
    reached = jnp.minimum(identity_mat + parent_mat, 1.0)
    for repeat in range(max(1, (tree_node_count - 1).bit_length())):
        step = reached.astype(jnp.bfloat16)
        reached = jnp.minimum(
            jnp.einsum("rnm,rmk->rnk", step, step, preferred_element_type=jnp.float32), 1.0
        )
    return reached


def pick_kernel(shifts, picked_ref, left_ref, down_ref, up_ref, left_out, *rest):
    firsts, seconds, sems = rest[:shifts], rest[shifts : 2 * shifts], rest[2 * shifts]
    half = up_ref.shape[2] // 2
    width = down_ref.shape[2]
    copies = []
    for shift in range(shifts):
        for slot in range(CAP):
            at = shift * CAP + slot
            index = picked_ref[at]
            pairs = (
                (up_ref.at[index, :, pl.ds(0, half)], firsts[shift].at[slot, :, pl.ds(0, half)]),
                (down_ref.at[index], firsts[shift].at[slot, :, pl.ds(half, width)]),
                (up_ref.at[index, :, pl.ds(half, half)], seconds[shift].at[slot]),
            )
            for which, (source, target) in enumerate(pairs):
                copies.append(pltpu.make_async_copy(source, target, sems.at[which, at]))
    for copy in copies:
        copy.start()
    for r in range(left_ref.shape[0]):
        left_out[r] = left_ref[r]
    for copy in copies:
        copy.wait()


def pick(picked, left, down, up):
    shifts = picked.shape[0] // CAP
    hbm = pl.BlockSpec(memory_space=pl.ANY)
    smem = pl.BlockSpec(memory_space=pltpu.SMEM)
    half = up.shape[2] // 2
    first = jax.ShapeDtypeStruct((CAP, up.shape[1], half + down.shape[2]), up.dtype)
    second = jax.ShapeDtypeStruct((CAP, up.shape[1], half), up.dtype)
    out = pl.pallas_call(
        functools.partial(pick_kernel, shifts),
        in_specs=[smem, smem, hbm, hbm],
        out_specs=[smem] + [hbm] * (2 * shifts),
        out_shape=[jax.ShapeDtypeStruct(left.shape, left.dtype)]
        + [first] * shifts
        + [second] * shifts,
        scratch_shapes=[pltpu.SemaphoreType.DMA((3, shifts * CAP))],
        compiler_params=params(),
        name="pick",
    )(picked, left, down, up)
    return out[0], out[1 : 1 + shifts], out[1 + shifts :]


def exchange(blocks, axis):
    size = len(blocks)
    got = [blocks[0]]
    for shift in range(1, size):
        pairs = [(i, (i + shift) % size) for i in range(size)]
        got.append(lax.ppermute(blocks[shift], axis, pairs))
    return got


def attend_kernel(blocks, meta_ref, *refs):
    q_refs = refs[:blocks]
    k_ref, v_ref = refs[blocks : blocks + 2]
    out_refs = refs[blocks + 2 :]
    _, nodes, width_here = q_refs[0].shape
    heads_here = width_here // HEAD_WIDTH
    request = pl.program_id(0)
    positions = k_ref.shape[1]
    left = meta_ref[request]
    rows = []
    for block in range(blocks):
        for head in range(heads_here):
            rows.append(q_refs[block][0, :, head * HEAD_WIDTH : (head + 1) * HEAD_WIDTH])
    query = jnp.concatenate(rows, axis=0)
    scores = dot(query, k_ref[0], CONTRACT_LAST) * INV_ROOT
    place = lax.broadcasted_iota(jnp.int32, (1, positions), 1)
    valid = place < left
    scores = jnp.where(valid, scores, NEG_FILL)
    top = jnp.max(scores, axis=1, keepdims=True).astype(jnp.bfloat16).astype(jnp.float32)
    weights = jnp.where(valid, jnp.exp(scores - top), 0.0)
    total = jnp.sum(weights, axis=1, keepdims=True)
    summed = dot(weights.astype(jnp.bfloat16), v_ref[0]).astype(jnp.bfloat16)
    high = total.astype(jnp.bfloat16).astype(jnp.float32)
    low = total - high
    lane = lax.broadcasted_iota(jnp.int32, (nodes, LANES), 1)
    for block in range(blocks):
        stats = jnp.zeros((nodes, LANES), jnp.float32)
        for head in range(heads_here):
            at = (block * heads_here + head) * nodes
            out_refs[block][head, 0] = summed[at : at + nodes]
            stats = jnp.where(lane == head, top[at : at + nodes], stats)
            stats = jnp.where(lane == heads_here + head, high[at : at + nodes], stats)
            stats = jnp.where(lane == 2 * heads_here + head, low[at : at + nodes], stats)
        out_refs[block][heads_here, 0] = stats.astype(jnp.bfloat16)


def attend(meta, queries, keys, values):
    blocks = len(queries)
    requests, nodes, width_here = queries[0].shape
    heads_here = width_here // HEAD_WIDTH
    prefix_here = keys.shape[1]
    out_block = (heads_here + 1, requests, nodes, HEAD_WIDTH)
    cache_spec = pl.BlockSpec((1, prefix_here, HEAD_WIDTH), lambda r, m: (r, 0, m[requests]))
    return pl.pallas_call(
        functools.partial(attend_kernel, blocks),
        grid_spec=pltpu.PrefetchScalarGridSpec(
            num_scalar_prefetch=1,
            grid=(requests,),
            in_specs=[pl.BlockSpec((1, nodes, width_here), lambda r, m: (r, 0, 0))] * blocks
            + [cache_spec, cache_spec],
            out_specs=[
                pl.BlockSpec((heads_here + 1, 1, nodes, HEAD_WIDTH), lambda r, m: (0, r, 0, 0))
            ]
            * blocks,
        ),
        out_shape=[jax.ShapeDtypeStruct(out_block, jnp.bfloat16)] * blocks,
        compiler_params=params(),
        cost_estimate=pl.CostEstimate(
            flops=4 * requests * nodes * width_here * blocks * prefix_here,
            bytes_accessed=4 * requests * prefix_here * HEAD_WIDTH,
            transcendentals=requests * nodes * heads_here * blocks * prefix_here,
        ),
        name="attend",
    )(meta, *queries, keys, values)


def merge_kernel(kv_ref, q_ref, tk_ref, tv_ref, linked_ref, *refs):
    got_refs, out_ref = refs[:-1], refs[-1]
    sources = len(got_refs)
    more, _, nodes, _ = got_refs[0].shape
    heads = more - 1
    query = jnp.concatenate(
        [q_ref[0, :, h * HEAD_WIDTH : (h + 1) * HEAD_WIDTH] for h in range(heads)], axis=0
    )
    linked = jnp.concatenate([linked_ref[0]] * heads, axis=0) > 0.5
    scores = dot(query, tk_ref[0], CONTRACT_LAST) * INV_ROOT
    top = jnp.max(jnp.where(linked, scores, NEG_FILL), axis=1, keepdims=True)
    tops, totals = [], []
    for source in range(sources):
        stats = got_refs[source][heads, 0].astype(jnp.float32)

        def columns(first):
            return jnp.concatenate([stats[:, first + h : first + h + 1] for h in range(heads)], axis=0)

        tops.append(columns(0))
        totals.append(columns(heads) + columns(2 * heads))
    for value in tops:
        top = jnp.maximum(top, value)
    weights = jnp.where(linked, jnp.exp(scores - top), 0.0)
    total = jnp.sum(weights, axis=1, keepdims=True)
    summed = dot(weights.astype(jnp.bfloat16), tv_ref[0])
    for source in range(sources):
        factor = jnp.exp(tops[source] - top)
        total = total + totals[source] * factor
        part = jnp.concatenate([got_refs[source][h, 0] for h in range(heads)], axis=0)
        summed = summed + part.astype(jnp.float32) * factor
    attended = (summed / total).astype(jnp.bfloat16)
    for h in range(heads):
        out_ref[0, :, h * HEAD_WIDTH : (h + 1) * HEAD_WIDTH] = attended[h * nodes : (h + 1) * nodes]


def merge(kv_group, got, queries, tree_keys, tree_values, linked):
    more, requests, nodes, _ = got[0].shape
    width_here = queries.shape[2]
    return pl.pallas_call(
        merge_kernel,
        grid_spec=pltpu.PrefetchScalarGridSpec(
            num_scalar_prefetch=1,
            grid=(requests,),
            in_specs=[
                pl.BlockSpec((1, nodes, width_here), lambda r, k: (r, 0, 0)),
                pl.BlockSpec((1, nodes, HEAD_WIDTH), lambda r, k: (r, 0, k[0])),
                pl.BlockSpec((1, nodes, HEAD_WIDTH), lambda r, k: (r, 0, k[0])),
                pl.BlockSpec((1, nodes, nodes), lambda r, k: (r, 0, 0)),
            ]
            + [pl.BlockSpec((more, 1, nodes, HEAD_WIDTH), lambda r, k: (0, r, 0, 0))] * len(got),
            out_specs=pl.BlockSpec((1, nodes, width_here), lambda r, k: (r, 0, 0)),
        ),
        out_shape=jax.ShapeDtypeStruct((requests, nodes, width_here), jnp.bfloat16),
        compiler_params=params(),
        name="merge",
    )(kv_group, queries, tree_keys, tree_values, linked, *got)


def project_kernel(slot_ref, x_ref, down_ref, w_ref, out_ref):
    requests, nodes, width_here = x_ref.shape
    wide = w_ref.shape[1]
    rows = x_ref[...].reshape(requests * nodes, width_here)
    out_ref[:, :wide] = dot(rows, w_ref[...]).astype(jnp.bfloat16)
    out_ref[:, wide:] = jnp.zeros((requests * nodes, LANES), jnp.bfloat16)
    for r in range(requests):
        part = dot(x_ref[r], down_ref[slot_ref[r]], CONTRACT_LAST)
        out_ref[r * nodes : (r + 1) * nodes, wide : wide + ADAPTER_RANK] = part.astype(jnp.bfloat16)


def project(meta, attended, maps, weight, columns):
    requests, nodes, width_here = attended.shape
    slots = maps.shape[0]
    down_block = maps.shape[2] // width_here - 1
    wide = weight.shape[1] // columns
    rows = requests * nodes
    return pl.pallas_call(
        project_kernel,
        grid_spec=pltpu.PrefetchScalarGridSpec(
            num_scalar_prefetch=1,
            grid=(1,),
            in_specs=[
                pl.BlockSpec((requests, nodes, width_here), lambda i, s: (0, 0, 0)),
                pl.BlockSpec((slots, ADAPTER_RANK, width_here), lambda i, s: (0, 0, down_block)),
                pl.BlockSpec((width_here, wide), lambda i, s: (0, s[requests])),
            ],
            out_specs=pl.BlockSpec((rows, wide + LANES), lambda i, s: (0, 0)),
        ),
        out_shape=jax.ShapeDtypeStruct((rows, wide + LANES), jnp.bfloat16),
        compiler_params=params(),
        cost_estimate=pl.CostEstimate(
            flops=2 * rows * width_here * wide,
            bytes_accessed=2 * width_here * wide,
            transcendentals=0,
        ),
        name="project",
    )(meta, attended, maps, weight)


def raise_kernel(slot_ref, first_ref, second_ref, *refs):
    share_refs, out_ref = refs[:-1], refs[-1]
    wide = out_ref.shape[2]
    half = wide // 2

    def added(start, size):
        total = share_refs[0][:, start : start + size].astype(jnp.float32)
        for share_ref in share_refs[1:]:
            total = total + share_ref[:, start : start + size].astype(jnp.float32)
        return total

    shrunk = added(wide, LANES)[:, :ADAPTER_RANK].astype(jnp.bfloat16)
    for at, up_ref in ((0, first_ref), (half, second_ref)):
        raised = dot(shrunk, up_ref[0])
        out_ref[0, :, at : at + half] = (added(at, half) + ADAPTER_SCALE * raised).astype(
            jnp.bfloat16
        )


def finish(slot_code, shares, maps, rest, requests):
    rows, wider = shares[0].shape
    wide = wider - LANES
    nodes = rows // requests
    up_spec = pl.BlockSpec((1, ADAPTER_RANK, wide // 2), lambda r, s: (s[r], 0, 0))
    share_spec = pl.BlockSpec((nodes, wider), lambda r, s: (r, 0))
    return pl.pallas_call(
        raise_kernel,
        grid_spec=pltpu.PrefetchScalarGridSpec(
            num_scalar_prefetch=1,
            grid=(requests,),
            in_specs=[up_spec, up_spec] + [share_spec] * len(shares),
            out_specs=pl.BlockSpec((1, nodes, wide), lambda r, s: (r, 0, 0)),
        ),
        out_shape=jax.ShapeDtypeStruct((requests, nodes, wide), jnp.bfloat16),
        compiler_params=params(),
        name="finish",
    )(slot_code, maps, rest, *shares)


def per_device(
    queries,
    prefix_key_cache,
    prefix_value_cache,
    tree_node_keys,
    tree_node_values,
    lengths,
    parents,
    request_adapter_index,
    output_projection_weight,
    adapter_down_weight,
    adapter_up_weight,
):
    requests, nodes, width_here = queries.shape
    columns = lax.axis_size("mp")
    column = lax.axis_index("mp")
    prefix_here = prefix_key_cache.shape[1]
    kv_heads = prefix_key_cache.shape[2] // HEAD_WIDTH
    batch_size = lax.axis_size("batch")
    batch_row = lax.axis_index("batch")
    present, rank, _ = adapter_down_weight.shape

    every_ids = request_adapter_index.reshape(batch_size, requests)
    is_mine = every_ids // present == batch_row
    counted = is_mine.astype(jnp.int32)
    slot_rank = jnp.cumsum(counted, axis=1) - counted
    slot_ids = jnp.arange(CAP, dtype=jnp.int32)
    select = (slot_rank[:, None, :] == slot_ids[None, :, None]) & is_mine[:, None, :]
    picked = jnp.sum(jnp.where(select, (every_ids % present)[:, None, :], 0), axis=2)
    target = (batch_row + jnp.arange(batch_size, dtype=jnp.int32)) % batch_size
    chosen = target[:, None] == jnp.arange(batch_size, dtype=jnp.int32)[None, :]
    picked = jnp.sum(jnp.where(chosen[:, :, None], picked[None], 0), axis=1).reshape(-1)
    left, firsts, seconds = pick(
        picked, lengths - column * prefix_here, adapter_down_weight, adapter_up_weight
    )
    maps = jnp.concatenate(exchange(firsts, "batch"), axis=0)
    rest = jnp.concatenate(exchange(seconds, "batch"), axis=0)
    mine_ids = lax.dynamic_slice_in_dim(request_adapter_index, batch_row * requests, requests)
    my_owner = mine_ids // present
    positions = jnp.arange(requests, dtype=jnp.int32)
    earlier = (my_owner[:, None] == my_owner[None, :]) & (positions[None, :] < positions[:, None])
    distance = (batch_row - my_owner + batch_size) % batch_size
    slot_code = distance * CAP + jnp.sum(earlier.astype(jnp.int32), axis=1)

    peers = columns // kv_heads
    own_group = column // peers

    def step(block, j, e):
        if j == 0 and e % peers == 0:
            return block
        pairs = [
            (i, (i // peers + j) % kv_heads * peers + (i % peers + e) % peers)
            for i in range(columns)
        ]
        return lax.ppermute(block, "mp", pairs)

    group_queries = [
        [step(queries, -j, -e) for e in range(peers)] for j in range(kv_heads)
    ]
    got = []
    for j in range(kv_heads):
        meta = jnp.concatenate([left, ((own_group + j) % kv_heads).reshape(1)])
        partial = attend(meta, group_queries[j], prefix_key_cache, prefix_value_cache)
        got.extend(step(partial[e], j, e) for e in range(peers))
    kv_group = own_group.reshape(1)
    attended = merge(
        kv_group, got, queries, tree_node_keys, tree_node_values, ancestors(parents)
    )
    shares = []
    for shift in range(columns):
        target_column = ((column + shift) % columns).reshape(1)
        project_meta = jnp.concatenate([slot_code, target_column])
        shares.append(project(project_meta, attended, maps, output_projection_weight, columns))
    return finish(slot_code, exchange(shares, "mp"), maps, rest, requests)


def solution(mesh):
    return jax.shard_map(
        per_device,
        mesh=mesh,
        in_specs=(
            P(("groups", "batch"), None, "mp"),
            P(("groups", "batch"), "mp", None),
            P(("groups", "batch"), "mp", None),
            P(("groups", "batch"), None, None),
            P(("groups", "batch"), None, None),
            P(("groups", "batch")),
            P(("groups", "batch"), None),
            P("groups"),
            P("mp", None),
            P("batch", None, "mp"),
            P("batch", None, "mp"),
        ),
        out_specs=P(("groups", "batch"), None, "mp"),
        check_vma=False,
    )
```
